128 devices in a mesh: outer: 8 (over y, x_lo), inner: 4 (over z), tensor: 4 (over x_hi, core).
Axes of the slice: x: 4 (x_hi: 2, x_lo: 2; x = x_hi * 2 + x_lo), y: 4, z: 4, core: 2. Of those that a mesh axis runs over, the one named last changes fastest.
Arguments:
- queries: bfloat16 [16384, 4096], P(('outer', 'inner'), 'tensor'), may hold values from -8 to 8
- keys: bfloat16 [16384, 512], P(('outer', 'inner'), 'tensor'), may hold values from -6 to 6
- values: bfloat16 [16384, 512], P(('outer', 'inner'), 'tensor'), may hold values from -6 to 6
- positions: int32 [16384], P(('outer', 'inner')), may hold values from 0 to 16383, as said below
- out_weight: bfloat16 [4096, 4096], P('tensor'), may hold values from -0.5 to 0.5
Outputs:
- projected: bfloat16 [16384, 4096], P(('outer', 'inner'))
The draws below stay inside these ranges and needn't reach their ends.
Inputs may be any that keep to these rules, and one draw needn't show every extreme that they name: Along outer+inner, each device's 512 stored tokens are two runs of 256 consecutive increasing positions, each run starting at a multiple of 256; every position from 0 to 16383 occurs exactly once.
All inputs are finite; a program needn't handle non-finite values.
Results may differ from the reference program's by a relative error of at most 0.018.
Values may be sent and summed in bfloat16 or wider, within the bound.
No kernel may reach another device: no remote copies, remote signals or barrier semaphores. Data moves between devices by JAX's collectives and lax.ppermute only.
A program may use at most 576 MiB of HBM per device.

```python
import jax
import jax.numpy as jnp
from jax import lax

QUERY_HEAD_COUNT = 32
KEY_VALUE_HEADS = 4
HEAD_DIMENSION = 128
DOUT = 4096
HALF = 256
SEQUENCE_TOKENS = 16384
N_OUTER = 8
N_INNER = 4


def draw_keys(key, part):
    key = jax.random.fold_in(key, 1)
    base_offset = jnp.clip(jax.random.normal(key, (SEQUENCE_TOKENS, KEY_VALUE_HEADS, HEAD_DIMENSION), jnp.float32), -6.0, 6.0)
    return base_offset.reshape(SEQUENCE_TOKENS, KEY_VALUE_HEADS * HEAD_DIMENSION).astype(jnp.bfloat16)


def draw_queries(key, part):
    key = jax.random.fold_in(key, 2)
    head_group = QUERY_HEAD_COUNT // KEY_VALUE_HEADS
    base_offset = jnp.clip(jax.random.normal(key, (SEQUENCE_TOKENS, KEY_VALUE_HEADS, head_group, HEAD_DIMENSION), jnp.float32), -6.0, 6.0)
    return base_offset.reshape(SEQUENCE_TOKENS, QUERY_HEAD_COUNT * HEAD_DIMENSION).astype(jnp.bfloat16)


def draw_positions(key, part):
    key = jax.random.fold_in(key, 3)
    runs = 2 * N_OUTER * N_INNER
    token_order = jax.random.permutation(key, runs).astype(jnp.int32)
    offsets = jnp.arange(HALF, dtype=jnp.int32)
    return (token_order[:, None] * HALF + offsets[None, :]).reshape(SEQUENCE_TOKENS).astype(jnp.int32)


def level_of(stream_key, dims, cuts, least, top_value):
    loudness = 1.0
    for dim, shards_of in cuts:
        draws = jax.random.uniform(jax.random.fold_in(jax.random.fold_in(stream_key, 6), dim), (shards_of,), jnp.float32, least / len(cuts), top_value / len(cuts))
        loudness = loudness * jnp.repeat(jnp.exp(draws), dims[dim] // shards_of).reshape((-1,) + (1,) * (len(dims) - 1 - dim))
    return loudness


def centred(own_key, extent, deviation, bound, cuts=(), kind=jnp.bfloat16):
    loudness = level_of(own_key, extent, cuts, -0.22, 0.18) if cuts else 1.0
    drawn = jax.random.normal(own_key, extent, jnp.float32) * deviation * loudness
    return jnp.minimum(jnp.maximum(drawn, -bound), bound).astype(kind)


def setup_inputs(seed: int = 0) -> dict:
    splits = jax.random.split(jax.random.key(seed), 6)
    queries = draw_queries(jax.random.fold_in(splits[5], 71), 0)
    keys = draw_keys(jax.random.fold_in(splits[5], 71), 0)
    values = centred(splits[2], (SEQUENCE_TOKENS, KEY_VALUE_HEADS * HEAD_DIMENSION), 1.0, 6.0, ((0, 32), (1, 4)))
    positions = draw_positions(jax.random.fold_in(splits[5], 71), 0)
    out_weight = centred(splits[4], (QUERY_HEAD_COUNT * HEAD_DIMENSION, DOUT), HEAD_DIMENSION ** -0.5, 0.5, ((0, 4),))
    return {"queries": queries, "keys": keys, "values": values, "positions": positions, "out_weight": out_weight}


def attend_block(query_tile, key_tile, value_tile, start, stop):
    scale = HEAD_DIMENSION ** -0.5
    rows = jnp.arange(start, stop, dtype=jnp.int32)
    cols = jnp.arange(0, stop, dtype=jnp.int32)
    keep = rows[:, None] >= cols[None, :]

    def single_head(index):
        qb = lax.dynamic_index_in_dim(query_tile, index, 0, False)[:, start:stop].astype(jnp.float32)
        kb = lax.dynamic_index_in_dim(key_tile, index, 0, False)[:stop].astype(jnp.float32)
        vb = lax.dynamic_index_in_dim(value_tile, index, 0, False)[:stop].astype(jnp.float32)
        score = jnp.einsum("gqd,kd->gqk", qb, kb) * scale
        score = jnp.where(keep[None], score, -jnp.inf)
        rowmax = jnp.max(score, axis=-1, keepdims=True)
        weight = jnp.where(keep[None], jnp.exp(score - rowmax), 0.0)
        total = jnp.sum(weight, axis=-1, keepdims=True)
        weight_b = weight.astype(jnp.bfloat16).astype(jnp.float32)
        mixed = jnp.einsum("gqk,kd->gqd", weight_b, vb)
        return (mixed / total).astype(jnp.bfloat16)

    head_list = lax.map(single_head, jnp.arange(KEY_VALUE_HEADS, dtype=jnp.int32))
    count = stop - start
    return head_list.transpose(2, 0, 1, 3).reshape(count, QUERY_HEAD_COUNT * HEAD_DIMENSION)


def reference(queries, keys, values, positions, out_weight):
    token_order = jnp.argsort(positions).astype(jnp.int32)
    head_group = QUERY_HEAD_COUNT // KEY_VALUE_HEADS
    query_tile = queries[token_order].reshape(SEQUENCE_TOKENS, KEY_VALUE_HEADS, head_group, HEAD_DIMENSION).transpose(1, 2, 0, 3)
    key_tile = keys[token_order].reshape(SEQUENCE_TOKENS, KEY_VALUE_HEADS, HEAD_DIMENSION).transpose(1, 0, 2)
    value_tile = values[token_order].reshape(SEQUENCE_TOKENS, KEY_VALUE_HEADS, HEAD_DIMENSION).transpose(1, 0, 2)
    block = min(512, SEQUENCE_TOKENS)
    pieces = []
    for start in range(0, SEQUENCE_TOKENS, block):
        pieces.append(attend_block(query_tile, key_tile, value_tile, start, start + block))
    ordered = jnp.concatenate(pieces, axis=0)
    attended = jnp.zeros_like(ordered).at[token_order].set(ordered)
    return jnp.dot(attended, out_weight, preferred_element_type=jnp.float32).astype(jnp.bfloat16)
```

```python
import functools
import math

import jax
import jax.numpy as jnp
import numpy as np
from jax import lax
from jax.experimental import pallas as pl
from jax.experimental.pallas import tpu as pltpu
from jax.sharding import Mesh
from jax.sharding import PartitionSpec as P

D = 128
RUN = 256
AXES = ("y", "xl", "z", "xh", "c")
SIZES = (4, 2, 4, 2, 2)
SCALE = math.log2(math.e) / math.sqrt(D)
ROWS = 528
NQ = 4096
PER = 1024
TILE = 512
UNROLL = 4
LIMIT = 100.0
VMEM = 56 * 2**20
EARLY, LATE = 16, 48
F32, BF16, I32 = jnp.float32, jnp.bfloat16, jnp.int32


def route(block, f):
    pairs = [
        (int(np.ravel_multi_index(i, SIZES)), int(np.ravel_multi_index(f(*i), SIZES)))
        for i in np.ndindex(*SIZES)
    ]
    return lax.ppermute(block, AXES, pairs)


def along_z(block, d):
    return route(block, lambda y, xl, z, xh, c: (y, xl, (z + d) % 4, xh, c))


def along_y(block, d):
    return route(block, lambda y, xl, z, xh, c: ((y + d) % 4, xl, z, xh, c))


def other_core(block):
    return route(block, lambda y, xl, z, xh, c: (y, xl, z, xh, 1 - c))


def values_of(kv, slot):
    ones = kv[slot, 512:528, :]
    return [jnp.concatenate([kv[slot, 256 + 128 * h : 384 + 128 * h, :], ones], axis=0) for h in (0, 1)]


def keys_of(kv, slot):
    return kv[slot, 0:256, :]


def work_list(order, items, ranks, base, count, rank, run, n, dummy):
    def put(s, found):
        order[found] = base + s
        return found + (ranks[base + s] < rank).astype(I32)

    found = lax.fori_loop(0, count, put, jnp.int32(0))
    order[found] = dummy

    def pair(p, n):
        items[0, n] = run
        items[1, n] = order[2 * p]
        items[2, n] = order[2 * p + 1]
        return n + 1

    return lax.fori_loop(0, (found + 1) // 2, pair, n)


def absorb_items(items, n, kv, qt, mref, acc, viol, dummy):
    for u in range(UNROLL):
        items[0, n + u] = 0
        items[1, n + u] = dummy
        items[2, n + u] = dummy

    @pl.loop(0, (n + UNROLL - 1) // UNROLL)
    def _(t):
        steps = []
        for u in range(UNROLL):
            run, a, b = (items[w, t * UNROLL + u] for w in range(3))
            k = jnp.concatenate([keys_of(kv, a), keys_of(kv, b)], axis=0)
            k = jnp.concatenate([k, k], axis=1)
            v = jnp.concatenate(values_of(kv, a) + values_of(kv, b), axis=1)
            for j in range(PER // TILE):
                cols = pl.ds(pl.multiple_of(run * PER + j * TILE, TILE), TILE)
                steps.append((k, v, cols))

        def score(i):
            k, _, cols = steps[i]
            return jnp.dot(k, qt[:, cols], preferred_element_type=F32)

        s = score(0)
        for i, (_, v, cols) in enumerate(steps):
            later = score(i + 1) if i + 1 < len(steps) else None
            x = s - mref[:, cols]
            viol[:, cols] = jnp.maximum(viol[:, cols], jnp.max(x.reshape(2 * RUN // 8, 8, TILE), axis=0))
            p = jnp.exp2(x).astype(BF16)
            acc[:, cols] += jnp.dot(v, p, preferred_element_type=F32)
            s = later


def fill(kv, base, sources, sems):
    copies = []
    for i, src in enumerate(sources):
        copy = pltpu.make_async_copy(src, kv.at[pl.ds(base, src.shape[0])], sems.at[i])
        copy.start()
        copies.append(copy)
        base += src.shape[0]
    return copies


def set_ones(kv, first, count):
    kv[pl.ds(first, count), 512:528, :] = jnp.ones((count, 16, D), BF16)


def early_kernel(ranks, q0, q1, s0, s1, qt, mref, acc, viol, kv, order, items, sems):
    copies = fill(kv, 0, (s0, s1), sems)
    for i in range(4):
        q = (q0, q1)[i // 2]
        for h in range(4):
            block = q[(i % 2) * RUN : (i % 2 + 1) * RUN, h * D : (h + 1) * D].astype(F32).T * SCALE
            high = block.astype(BF16)
            cols = slice(i * PER + h * RUN, i * PER + (h + 1) * RUN)
            qt[0:D, cols] = high
            qt[D : 2 * D, cols] = (block - high.astype(F32)).astype(BF16)
    n = jnp.int32(0)
    for i in range(4):
        n = work_list(order, items, ranks, 0, EARLY, ranks[4 * i], i, n, EARLY)
    for copy in copies:
        copy.wait()
    set_ones(kv, 0, EARLY)
    kv[EARLY] = jnp.zeros((ROWS, D), BF16)
    key = lax.broadcasted_iota(I32, (RUN, PER), 0)
    query = lax.broadcasted_iota(I32, (RUN, PER), 1) % RUN
    keep = key <= query
    for i in range(4):
        cols = slice(i * PER, (i + 1) * PER)
        k = keys_of(kv, 4 * i)
        s = jnp.dot(jnp.concatenate([k, k], axis=1), qt[:, cols], preferred_element_type=F32)
        s = jnp.where(keep, s, -1e30)
        top = jnp.max(s, axis=0, keepdims=True)
        mref[:, cols] = top
        p = jnp.exp2(s - top).astype(BF16)
        v = jnp.concatenate(values_of(kv, 4 * i), axis=1)
        acc[:, cols] = jnp.dot(v, p, preferred_element_type=F32)
    viol[...] = jnp.zeros_like(viol)
    absorb_items(items, n, kv, qt, mref, acc, viol, EARLY)


def late_kernel(count, ranks, qt, mref, acc_in, viol_in, *rest):
    early, late = rest[:2], rest[2 : 2 + count]
    out, kv, acc, viol, order, items, sems = rest[2 + count :]
    dummy = EARLY + LATE
    copies = fill(kv, EARLY, late, sems)
    n = jnp.int32(0)
    for i in range(4):
        n = work_list(order, items, ranks, EARLY, LATE, ranks[4 * i], i, n, dummy)
    acc[...] = acc_in[...]
    viol[...] = viol_in[...]
    for copy in copies:
        copy.wait()
    set_ones(kv, EARLY, LATE)
    kv[dummy] = jnp.zeros((ROWS, D), BF16)
    absorb_items(items, n, kv, qt, mref, acc, viol, dummy)

    @pl.when(jnp.max(viol[...]) > LIMIT)
    def _():
        for copy in fill(kv, 0, early, sems):
            copy.wait()
        set_ones(kv, 0, EARLY)
        later = lax.broadcasted_iota(I32, (RUN, RUN), 0) > lax.broadcasted_iota(I32, (RUN, RUN), 1)

        @pl.loop(0, NQ // RUN)
        def _(t):
            cols = pl.ds(pl.multiple_of(t * RUN, RUN), RUN)
            rank = ranks[4 * (t // (PER // RUN))]
            acc[:, cols] = jnp.zeros((144, RUN), F32)
            viol[:, cols] = jnp.full((8, RUN), -1e30, F32)

            @pl.loop(0, EARLY + LATE)
            def _(slot):
                @pl.when(ranks[slot] <= rank)
                def _():
                    k = keys_of(kv, slot)
                    s = jnp.dot(jnp.concatenate([k, k], axis=1), qt[:, cols], preferred_element_type=F32)
                    drop = jnp.logical_and(later, jnp.full((RUN, RUN), ranks[slot], I32) == rank)
                    s = jnp.where(drop, -1e30, s)
                    old = viol[0:1, cols]
                    top = jnp.maximum(old, jnp.max(s, axis=0, keepdims=True))
                    viol[0:1, cols] = top
                    p = jnp.exp2(s - top).astype(BF16)
                    v = jnp.concatenate(values_of(kv, slot), axis=1)
                    acc[:, cols] = acc[:, cols] * jnp.exp2(old - top) + jnp.dot(v, p, preferred_element_type=F32)

    for i in range(4):
        for h in range(4):
            cols = slice(i * PER + h * RUN, i * PER + (h + 1) * RUN)
            block = acc[0:D, cols] / acc[D : D + 1, cols]
            out[i, :, h * D : (h + 1) * D] = block.T.astype(BF16)


def ranks_of(block):
    return block[:, 512, 0].astype(F32).astype(I32)


def attend(q0, q1, early, late):
    any_, vmem, smem = (pl.BlockSpec(memory_space=m) for m in (pl.ANY, pltpu.VMEM, pltpu.SMEM))
    ranks = jnp.concatenate([ranks_of(b) for b in early + late])
    pair = 8 * D * D
    params = pltpu.CompilerParams(vmem_limit_bytes=VMEM)
    qt, mref, acc, viol = pl.pallas_call(
        early_kernel,
        name="attend_early",
        out_shape=(
            jax.ShapeDtypeStruct((2 * D, NQ), BF16),
            jax.ShapeDtypeStruct((1, NQ), F32),
            jax.ShapeDtypeStruct((144, NQ), F32),
            jax.ShapeDtypeStruct((8, NQ), F32),
        ),
        in_specs=[smem, vmem, vmem, any_, any_],
        out_specs=(vmem,) * 4,
        scratch_shapes=[
            pltpu.VMEM((EARLY + 1, ROWS, D), BF16),
            pltpu.SMEM((EARLY + 8,), I32),
            pltpu.SMEM((3, 2 * EARLY + 16), I32),
            pltpu.SemaphoreType.DMA((2,)),
        ],
        compiler_params=params,
        cost_estimate=pl.CostEstimate(flops=8 * 10**9, bytes_accessed=8 * 10**6, transcendentals=16 * 10**6),
    )(jnp.concatenate([ranks_of(b) for b in early]), q0, q1, *early)
    return pl.pallas_call(
        functools.partial(late_kernel, len(late)),
        name="attend_late",
        out_shape=jax.ShapeDtypeStruct((4, RUN, 4 * D), BF16),
        in_specs=[smem] + [vmem] * 4 + [any_] * (2 + len(late)),
        out_specs=vmem,
        scratch_shapes=[
            pltpu.VMEM((EARLY + LATE + 1, ROWS, D), BF16),
            pltpu.VMEM((144, NQ), F32),
            pltpu.VMEM((8, NQ), F32),
            pltpu.SMEM((LATE + 8,), I32),
            pltpu.SMEM((3, 2 * LATE + 16), I32),
            pltpu.SemaphoreType.DMA((len(late),)),
        ],
        compiler_params=params,
        cost_estimate=pl.CostEstimate(flops=24 * 10**9, bytes_accessed=16 * 10**6, transcendentals=48 * 10**6),
    )(ranks, qt, mref, acc, viol, *early, *late)


def body(queries, keys, values, positions, out_weight):
    xl, c = lax.axis_index("xl"), lax.axis_index("c")
    rank = (positions.reshape(2, RUN)[:, 0] // RUN).astype(BF16)
    turned = values.reshape(2, 2, D, D).transpose(0, 1, 3, 2).reshape(2, RUN, D)
    marks = jnp.broadcast_to(rank[:, None, None], (2, 16, D))
    piece = jnp.concatenate([keys.reshape(2, RUN, D), turned, marks], axis=1)
    piece = route(piece, lambda y, xl, z, xh, c: (y, c, z, xh, xl))
    q = []
    for k in (0, 1):
        half = lax.dynamic_slice_in_dim(queries, (xl ^ k) * 4 * D, 4 * D, 1)
        q.append(route(half, lambda y, xl, z, xh, c, k=k: (y, c, z, xh, xl ^ k)))
    first, second = piece[0:1], piece[1:2]
    by_z = jnp.concatenate([first] + [along_z(first, d) for d in (1, 3, 2)])
    by_y = jnp.concatenate([second] + [along_y(second, d) for d in (1, 3, 2)])
    mine = jnp.concatenate([by_z, by_y])
    early = [mine, other_core(mine)]
    late = [f(b, d) for d in (1, 3, 2) for f, b in ((along_y, by_z), (along_z, by_y))]
    late = late + [other_core(b) for b in late]
    attended = attend(q[0], q[1], early, late)
    got = [
        route(attended[2 * k : 2 * k + 2].reshape(2 * RUN, 4 * D), lambda y, xl, z, xh, c, k=k: (y, c ^ k, z, xh, xl))
        for k in (0, 1)
    ]
    even = xl == 0
    mixed = jnp.concatenate([jnp.where(even, got[0], got[1]), jnp.where(even, got[1], got[0])], axis=1)
    part = jnp.dot(mixed, out_weight, preferred_element_type=F32).astype(BF16)
    width = part.shape[1] // 2
    keep = lax.dynamic_slice_in_dim(part, c * width, width, 1)
    give = lax.dynamic_slice_in_dim(part, (1 - c) * width, width, 1)
    half = (keep.astype(F32) + other_core(give).astype(F32)).astype(BF16)
    far = route(half, lambda y, xl, z, xh, c: (y, xl, z, 1 - xh, c))
    half = (half.astype(F32) + far.astype(F32)).astype(BF16)
    rest = other_core(half)
    low = c == 0
    return jnp.concatenate([jnp.where(low, half, rest), jnp.where(low, rest, half)], axis=1)


def solution(mesh):
    fine = Mesh(mesh.devices.reshape(SIZES), AXES)
    tokens, heads = ("y", "xl", "z"), ("xh", "c")
    placed = (P(tokens, heads), P(tokens, heads), P(tokens, heads), P(tokens), P(heads, None))
    return jax.shard_map(body, mesh=fine, in_specs=placed, out_specs=P(tokens, None), check_vma=False)
```

```python
import functools
import math

import jax
import jax.numpy as jnp
import numpy as np
from jax import lax
from jax.experimental import pallas as pl
from jax.experimental.pallas import tpu as pltpu
from jax.sharding import Mesh
from jax.sharding import PartitionSpec as P

D = 128
RUN = 256
AXES = ("y", "xl", "z", "xh", "c")
SIZES = (4, 2, 4, 2, 2)
SCALE = math.log2(math.e) / math.sqrt(D)
ROWS = 528
NQ = 4096
PER = 1024
TILE = 512
UNROLL = 4
LIMIT = 100.0
SHIFTS = (0, 1, 3, 2)
SHARE = 256
SHARE = 256
OWN = (0, 8, 1, 9)
VMEM = 28 * 2**20
PART = 16
PER = 1024
TILE = 512
UNROLL = 4
LIMIT = 100.0
SHIFTS = (0, 1, 3, 2)
SHARE = 256
OWN = (0, 8, 1, 9)
VMEM = 28 * 2**20
F32, BF16, I32 = jnp.float32, jnp.bfloat16, jnp.int32


def route(block, f):
    pairs = [
        (int(np.ravel_multi_index(i, SIZES)), int(np.ravel_multi_index(f(*i), SIZES)))
        for i in np.ndindex(*SIZES)
    ]
    return lax.ppermute(block, AXES, pairs)


def onward(block, d, stage):
    def f(y, xl, z, xh, c):
        return (y, xl, (z + d) % 4, xh, c) if c == stage else ((y + d) % 4, xl, z, xh, c)

    return route(block, f)


def other_core(block):
    return route(block, lambda y, xl, z, xh, c: (y, xl, z, xh, 1 - c))


def values_of(kv, slot):
    ones = kv[slot, 512:528, :]
    return [jnp.concatenate([kv[slot, 256 + 128 * h : 384 + 128 * h, :], ones], axis=0) for h in (0, 1)]


def keys_of(kv, slot):
    return kv[slot, 0:256, :]


def work_list(order, items, ranks, count, rank, run, n):
    def put(s, found):
        order[found] = s
        return found + (ranks[s] < rank).astype(I32)

    found = lax.fori_loop(0, count, put, jnp.int32(0))
    order[found] = count

    def pair(p, n):
        items[0, n] = run
        items[1, n] = order[2 * p]
        items[2, n] = order[2 * p + 1]
        return n + 1

    return lax.fori_loop(0, (found + 1) // 2, pair, n)


def absorb_items(items, n, kv, base, count, qt, mref, acc, viol):
    for u in range(UNROLL):
        items[0, n + u] = 0
        items[1, n + u] = count
        items[2, n + u] = count

    @pl.loop(0, (n + UNROLL - 1) // UNROLL)
    def _(t):
        steps = []
        for u in range(UNROLL):
            run, a, b = (items[w, t * UNROLL + u] for w in range(3))
            a, b = a + base, b + base
            k = jnp.concatenate([keys_of(kv, a), keys_of(kv, b)], axis=0)
            k = jnp.concatenate([k, k], axis=1)
            v = jnp.concatenate(values_of(kv, a) + values_of(kv, b), axis=1)
            steps += [(k, v, run, slice(j * TILE, (j + 1) * TILE)) for j in range(PER // TILE)]

        def score(i):
            k, _, run, cols = steps[i]
            return jnp.dot(k, qt[run, :, cols], preferred_element_type=F32)

        s = score(0)
        for i, (_, v, run, cols) in enumerate(steps):
            later = score(i + 1) if i + 1 < len(steps) else None
            x = s - mref[run, :, cols]
            viol[run, :, cols] = jnp.maximum(viol[run, :, cols], jnp.max(x.reshape(2 * RUN // 8, 8, TILE), axis=0))
            p = jnp.exp2(x).astype(BF16)
            acc[run, :, cols] += jnp.dot(v, p, preferred_element_type=F32)
            s = later


def read_ranks(kv, base, count, ranks):
    for s in range(count):
        ranks[s] = jnp.max(kv[base + s, 512:528, :].astype(F32)).astype(I32)


def fill(kv, base, sources, sems):
    copies = []
    for i, src in enumerate(sources):
        copy = pltpu.make_async_copy(src, kv.at[pl.ds(base, src.shape[0])], sems.at[i])
        copy.start()
        copies.append(copy)
        base += src.shape[0]
    return copies


def set_ones(kv, first, count):
    kv[pl.ds(first, count), 512:528, :] = jnp.ones((count, 16, D), BF16)


def turn_kernel(q0, q1, qt):
    for i in range(4):
        for h in range(4):
            rows = slice(i // 2 * RUN, (i // 2 + 1) * RUN)
            block = (q0, q1)[i % 2][rows, h * D : (h + 1) * D].astype(F32).T * SCALE
            high = block.astype(BF16)
            here = slice(h * RUN, (h + 1) * RUN)
            qt[i, 0:D, here] = high
            qt[i, D : 2 * D, here] = (block - high.astype(F32)).astype(BF16)


def early_kernel(qt, s0, s1, ranks, mref, acc, viol, kv, order, items, sems):
    for copy in fill(kv, 0, (s0, s1), sems):
        copy.wait()
    read_ranks(kv, 0, PART, ranks)
    n = jnp.int32(0)
    for i in range(4):
        n = work_list(order, items, ranks, PART, ranks[OWN[i]], i, n)
    set_ones(kv, 0, PART)
    kv[PART] = jnp.zeros((ROWS, D), BF16)
    key = lax.broadcasted_iota(I32, (RUN, PER), 0)
    query = lax.broadcasted_iota(I32, (RUN, PER), 1) % RUN
    keep = key <= query
    for i in range(4):
        k = keys_of(kv, OWN[i])
        s = jnp.dot(jnp.concatenate([k, k], axis=1), qt[i], preferred_element_type=F32)
        s = jnp.where(keep, s, -1e30)
        top = jnp.max(s, axis=0, keepdims=True)
        mref[i] = top
        p = jnp.exp2(s - top).astype(BF16)
        v = jnp.concatenate(values_of(kv, OWN[i]), axis=1)
        acc[i] = jnp.dot(v, p, preferred_element_type=F32)
    viol[...] = jnp.zeros_like(viol)
    absorb_items(items, n, kv, 0, PART, qt, mref, acc, viol)


def take_state(state, held, first, count, sems):
    copies = []
    for i, (src, dst) in enumerate(zip(state, held)):
        copy = pltpu.make_async_copy(src.at[pl.ds(first, count)], dst, sems.at[i])
        copy.start()
        copies.append(copy)
    return copies


def middle_kernel(early_ranks, qt, mref, acc_in, viol_in, s0, s1, ranks, acc, viol, kv, order, items, sems):
    copies = fill(kv, 0, (s0, s1), sems)
    acc[...] = acc_in[...]
    viol[...] = viol_in[...]
    for copy in copies:
        copy.wait()
    read_ranks(kv, 0, PART, ranks)
    n = jnp.int32(0)
    for i in range(4):
        n = work_list(order, items, ranks, PART, early_ranks[OWN[i]], i, n)
    set_ones(kv, 0, PART)
    kv[PART] = jnp.zeros((ROWS, D), BF16)
    absorb_items(items, n, kv, 0, PART, qt, mref, acc, viol)


def late_kernel(chunk, early_ranks, middle_ranks, *rest):
    state, sources = rest[:4], rest[4:12]
    *out, kv, qt, mref, acc, viol, ranks, order, items, sems, state_sems = rest[12:]
    base, count = 2 * PART, 2 * PART
    copies = fill(kv, base, sources[4:], sems)
    copies += take_state(state, (qt, mref, acc, viol), 2 * chunk, 2, state_sems)
    for copy in copies:
        copy.wait()
    read_ranks(kv, base, count, ranks)
    n = jnp.int32(0)
    for i in range(2):
        n = work_list(order, items, ranks, count, early_ranks[OWN[2 * chunk + i]], i, n)
    set_ones(kv, base, count)
    kv[base + count] = jnp.zeros((ROWS, D), BF16)
    absorb_items(items, n, kv, base, count, qt, mref, acc, viol)

    @pl.when(jnp.max(viol[...]) > LIMIT)
    def _():
        for copy in fill(kv, 0, sources[:4], sems):
            copy.wait()
        set_ones(kv, 0, base)
        later = lax.broadcasted_iota(I32, (RUN, RUN), 0) > lax.broadcasted_iota(I32, (RUN, RUN), 1)

        def take(slot, slot_rank, run, rank, cols):
            @pl.when(slot_rank <= rank)
            def _():
                k = keys_of(kv, slot)
                s = jnp.dot(jnp.concatenate([k, k], axis=1), qt[run, :, cols], preferred_element_type=F32)
                drop = jnp.logical_and(later, jnp.full((RUN, RUN), slot_rank, I32) == rank)
                s = jnp.where(drop, -1e30, s)
                old = viol[run, 0:1, cols]
                top = jnp.maximum(old, jnp.max(s, axis=0, keepdims=True))
                viol[run, 0:1, cols] = top
                p = jnp.exp2(s - top).astype(BF16)
                v = jnp.concatenate(values_of(kv, slot), axis=1)
                term = jnp.dot(v, p, preferred_element_type=F32)
                acc[run, :, cols] = acc[run, :, cols] * jnp.exp2(old - top) + term

        @pl.loop(0, 2 * PER // RUN)
        def _(t):
            run = t // (PER // RUN)
            cols = pl.ds(pl.multiple_of(t % (PER // RUN) * RUN, RUN), RUN)
            rank = jnp.where(run == 0, early_ranks[OWN[2 * chunk]], early_ranks[OWN[2 * chunk + 1]])
            acc[run, :, cols] = jnp.zeros((144, RUN), F32)
            viol[run, :, cols] = jnp.full((8, RUN), -1e30, F32)
            for first, held, many in ((0, early_ranks, PART), (PART, middle_ranks, PART), (base, ranks, count)):

                @pl.loop(0, many)
                def _(s, first=first, held=held):
                    take(first + s, held[s], run, rank, cols)

    for i in range(2):
        for h in range(4):
            cols = slice(h * RUN, (h + 1) * RUN)
            block = acc[i, 0:D, cols] / acc[i, D : D + 1, cols]
            out[i][:, h * D : (h + 1) * D] = block.T.astype(BF16)


def spec(space):
    return pl.BlockSpec(memory_space=space)


def cost(slots, runs):
    pairs = slots * RUN * runs * PER // 2
    return pl.CostEstimate(flops=8 * D * pairs, bytes_accessed=12 * 10**6, transcendentals=pairs)


RANKS = jax.ShapeDtypeStruct((PART,), I32)
def held(runs):
    return [pltpu.VMEM((runs, 2 * D, PER), BF16), pltpu.VMEM((runs, 1, PER), F32)]


STATE = (jax.ShapeDtypeStruct((4, 144, PER), F32), jax.ShapeDtypeStruct((4, 8, PER), F32))
PARAMS = pltpu.CompilerParams(vmem_limit_bytes=VMEM)
LARGE = pltpu.CompilerParams(vmem_limit_bytes=56 * 2**20)
SMALL = pltpu.CompilerParams(vmem_limit_bytes=12 * 2**20)


def lists(slots):
    return [pltpu.SMEM((slots + 8,), I32), pltpu.SMEM((3, 2 * slots + 16), I32)]


def turn(q0, q1):
    return pl.pallas_call(
        turn_kernel,
        name="turn_queries",
        out_shape=jax.ShapeDtypeStruct((4, 2 * D, PER), BF16),
        in_specs=[spec(pltpu.VMEM)] * 2,
        out_specs=spec(pltpu.VMEM),
        compiler_params=SMALL,
        cost_estimate=pl.CostEstimate(flops=10**7, bytes_accessed=3 * 10**6, transcendentals=0),
    )(q0, q1)


def attend_early(qt, pieces):
    return pl.pallas_call(
        early_kernel,
        name="attend_early",
        out_shape=(RANKS, jax.ShapeDtypeStruct((4, 1, PER), F32)) + STATE,
        in_specs=[spec(pltpu.VMEM)] + [spec(pl.ANY)] * 2,
        out_specs=(spec(pltpu.SMEM),) + (spec(pltpu.VMEM),) * 3,
        scratch_shapes=[pltpu.VMEM((PART + 1, ROWS, D), BF16), *lists(PART), pltpu.SemaphoreType.DMA((2,))],
        compiler_params=PARAMS,
        cost_estimate=cost(PART, 4),
    )(qt, *pieces)


def attend_middle(early_ranks, state, pieces):
    return pl.pallas_call(
        middle_kernel,
        name="attend_middle",
        out_shape=(RANKS,) + STATE,
        in_specs=[spec(pltpu.SMEM)] + [spec(pltpu.VMEM)] * 4 + [spec(pl.ANY)] * 2,
        out_specs=(spec(pltpu.SMEM),) + (spec(pltpu.VMEM),) * 2,
        scratch_shapes=[pltpu.VMEM((PART + 1, ROWS, D), BF16), *lists(PART), pltpu.SemaphoreType.DMA((2,))],
        compiler_params=PARAMS,
        cost_estimate=cost(PART, 4),
    )(early_ranks, *state, *pieces)


def attend_late(ranks, state, pieces, chunk):
    return pl.pallas_call(
        functools.partial(late_kernel, chunk),
        name="attend_late",
        out_shape=(jax.ShapeDtypeStruct((RUN, 4 * D), BF16),) * 2,
        in_specs=[spec(pltpu.SMEM)] * 2 + [spec(pl.ANY)] * 12,
        out_specs=(spec(pltpu.VMEM),) * 2,
        scratch_shapes=[
            pltpu.VMEM((4 * PART + 1, ROWS, D), BF16),
            *held(2),
            pltpu.VMEM((2, 144, PER), F32),
            pltpu.VMEM((2, 8, PER), F32),
            pltpu.SMEM((2 * PART,), I32),
            *lists(2 * PART),
            pltpu.SemaphoreType.DMA((4,)),
            pltpu.SemaphoreType.DMA((4,)),
        ],
        compiler_params=LARGE,
        cost_estimate=cost(2 * PART, 2),
    )(*ranks, *state, *pieces)


def project_kernel(place, even, a0, a1, b0, b1, w_own, w0, w1, w2, w3, out, rows, v_own, v_far, sems):
    width = w0.shape[1]
    copies = []
    for e, w in enumerate((w0, w1, w2, w3)):
        at = pl.ds(pl.multiple_of(place[e] * width, width), width)
        pair = (
            pltpu.make_async_copy(w_own.at[:, at], v_own.at[e], sems.at[2 * e]),
            pltpu.make_async_copy(w, v_far.at[e], sems.at[2 * e + 1]),
        )
        for copy in pair:
            copy.start()
        copies.append(pair)
    half = a0.shape[1]
    for swap in (0, 1):

        @pl.when(even[0] == 1 - swap)
        def _(swap=swap):
            for i, pair in enumerate(((a0, a1), (b0, b1))):
                rows[i, :, 0:half] = pair[swap][...]
                rows[i, :, half : 2 * half] = pair[1 - swap][...]

    for e in range(4):
        for copy in copies[e]:
            copy.wait()
        for j in range(width // SHARE):
            cols = slice(j * SHARE, (j + 1) * SHARE)
            term = jnp.dot(rows[0], v_own[e, :, cols], preferred_element_type=F32)
            term = term + jnp.dot(rows[1], v_far[e, :, cols], preferred_element_type=F32)
            at = pl.ds(pl.multiple_of(place[e] * width + j * SHARE, SHARE), SHARE)
            out[:, at] = term.astype(BF16)


def project(place, even, got, w_own, shares):
    rows, depth = got[0].shape[0], w_own.shape[0]
    width = w_own.shape[1]
    return pl.pallas_call(
        project_kernel,
        name="project",
        out_shape=jax.ShapeDtypeStruct((rows, width), BF16),
        in_specs=[spec(pltpu.SMEM)] * 2 + [spec(pltpu.VMEM)] * 4 + [spec(pl.ANY)] * 5,
        out_specs=spec(pltpu.VMEM),
        scratch_shapes=[
            pltpu.VMEM((2, rows, depth), BF16),
            pltpu.VMEM((4, depth, width // 4), BF16),
            pltpu.VMEM((4, depth, width // 4), BF16),
            pltpu.SemaphoreType.DMA((8,)),
        ],
        compiler_params=LARGE,
        cost_estimate=pl.CostEstimate(
            flops=4 * rows * depth * width, bytes_accessed=20 * 10**6, transcendentals=0
        ),
    )(place, even, *got, w_own, *shares)


def finish_kernel(a, b, *rest):
    rest[-1][...] = (a[...].astype(F32) + b[...].astype(F32)).astype(BF16)


def finish(a, b, chunk, before=None):
    rows, width = a.shape
    whole = pl.BlockSpec((rows // 4, width), lambda i: (i, 0))
    more = {} if before is None else {"input_output_aliases": {2: 0}}
    extra = [] if before is None else [before]
    return pl.pallas_call(
        finish_kernel,
        name="finish",
        grid=(4,),
        out_shape=jax.ShapeDtypeStruct((2 * rows, width), BF16),
        in_specs=[whole, whole] + [spec(pl.ANY)] * len(extra),
        out_specs=pl.BlockSpec((rows // 4, width), lambda i: (4 * chunk + i, 0)),
        compiler_params=SMALL,
        **more,
    )(a, b, *extra)


def body(queries, keys, values, positions, out_weight):
    xl, c = lax.axis_index("xl"), lax.axis_index("c")
    y, z = lax.axis_index("y"), lax.axis_index("z")
    rank = (positions.reshape(2, RUN)[:, 0] // RUN).astype(BF16)
    turned = values.reshape(2, 2, D, D).transpose(0, 1, 3, 2).reshape(2, RUN, D)
    marks = jnp.broadcast_to(rank[:, None, None], (2, 16, D))
    piece = jnp.concatenate([keys.reshape(2, RUN, D), turned, marks], axis=1)
    width = out_weight.shape[1] // 8
    line, bit = jnp.where(c == 0, y, z), jnp.where(c == 0, z, y) % 2
    share = lax.dynamic_slice_in_dim(out_weight, (line * 2 + bit) * width, width, 1)
    piece = route(piece, lambda y, xl, z, xh, c: (y, c, z, xh, xl))
    share = route(share, lambda y, xl, z, xh, c: (y, 1 - xl, z, 1 - xh, c))
    q = []
    for k in (0, 1):
        half = lax.dynamic_slice_in_dim(queries, (xl ^ k) * 4 * D, 4 * D, 1)
        q.append(route(half, lambda y, xl, z, xh, c, k=k: (y, c, z, xh, xl ^ k)))
    near = jnp.concatenate([piece] + [onward(piece, d, 0) for d in SHIFTS[1:]])
    near, q = lax.optimization_barrier((near, q))
    pieces = [near, other_core(near)]
    side = [onward(near, d, 1) for d in SHIFTS[1:]]
    qt = turn(*q)
    ranks, mref, acc, viol = attend_early(qt, pieces)
    side, acc, share = lax.optimization_barrier((side, acc, share))
    other = [other_core(b) for b in side]
    pair = route(share, lambda y, xl, z, xh, c: (y ^ c, xl, z ^ (1 - c), xh, c))
    more, acc, viol = attend_middle(ranks, (qt, mref, acc, viol), side[:2])
    other, acc, share, pair = lax.optimization_barrier((other, acc, share, pair))
    share = jnp.concatenate([jnp.where(bit == 0, share, pair), jnp.where(bit == 0, pair, share)], axis=1)
    shares = [share] + [onward(share, d, 1) for d in (1, 3)]
    pieces = [*pieces, *side, *other]
    place = (line - jnp.array(SHIFTS, I32)) % 4
    even = (xl == 0).astype(I32).reshape(1)
    state = (qt, mref, acc, viol)
    out = None
    for chunk in (0, 1):
        attended = attend_late((ranks, more), state, pieces, chunk)
        got = [
            route(attended[k], lambda y, xl, z, xh, c, k=k, far=far: (y, c ^ k, z, xh ^ far, xl))
            for far in (0, 1)
            for k in (0, 1)
        ]
        if chunk == 0:
            attended, state, shares = lax.optimization_barrier((attended, state, shares))
            shares.append(onward(shares[0], 2, 1))
        part = project(place, even, got, out_weight, shares)
        out = finish(part, other_core(part), chunk, out)
    return out


def solution(mesh):
    fine = Mesh(mesh.devices.reshape(SIZES), AXES)
    tokens, heads = ("y", "xl", "z"), ("xh", "c")
    placed = (P(tokens, heads), P(tokens, heads), P(tokens, heads), P(tokens), P(heads, None))
    return jax.shard_map(body, mesh=fine, in_specs=placed, out_specs=P(tokens, None), check_vma=False)
```

```python
import functools
import math

import jax
import jax.numpy as jnp
import numpy as np
from jax import lax
from jax.experimental import pallas as pl
from jax.experimental.pallas import tpu as pltpu
from jax.sharding import Mesh
from jax.sharding import PartitionSpec as P

D = 128
RUN = 256
AXES = ("y", "xl", "z", "xh", "c")
SIZES = (4, 2, 4, 2, 2)
SCALE = math.log2(math.e) / math.sqrt(D)
ROWS = 528
NQ = 4096
PER = 1024
TILE = 512
UNROLL = 4
LIMIT = 100.0
SHIFTS = (0, 1, 3, 2)
SHARE = 256
SHARE = 256
OWN = (0, 8, 1, 9)
VMEM = 28 * 2**20
PART = 16
PER = 1024
TILE = 512
UNROLL = 4
LIMIT = 100.0
SHIFTS = (0, 1, 3, 2)
SHARE = 256
OWN = (0, 8, 1, 9)
VMEM = 28 * 2**20
F32, BF16, I32 = jnp.float32, jnp.bfloat16, jnp.int32


def route(block, f):
    pairs = [
        (int(np.ravel_multi_index(i, SIZES)), int(np.ravel_multi_index(f(*i), SIZES)))
        for i in np.ndindex(*SIZES)
    ]
    return lax.ppermute(block, AXES, pairs)


def onward(block, d, stage):
    def f(y, xl, z, xh, c):
        return (y, xl, (z + d) % 4, xh, c) if c == stage else ((y + d) % 4, xl, z, xh, c)

    return route(block, f)


def other_core(block):
    return route(block, lambda y, xl, z, xh, c: (y, xl, z, xh, 1 - c))


def values_of(kv, slot):
    ones = kv[slot, 512:528, :]
    return [jnp.concatenate([kv[slot, 256 + 128 * h : 384 + 128 * h, :], ones], axis=0) for h in (0, 1)]


def keys_of(kv, slot):
    return kv[slot, 0:256, :]


def work_list(items, ranks, count, rank, run, n):
    found = jnp.int32(0)
    for s in range(count):
        items[0, n + (found >> 1)] = run
        items[1 + (found & 1), n + (found >> 1)] = s
        found = found + (ranks[s] < rank).astype(I32)
    items[1 + (found & 1), n + (found >> 1)] = count
    return n + ((found + 1) >> 1)


def absorb_items(items, n, kv, base, count, qt, mref, acc, viol):
    for u in range(UNROLL):
        items[0, n + u] = 0
        items[1, n + u] = count
        items[2, n + u] = count

    @pl.loop(0, (n + UNROLL - 1) // UNROLL)
    def _(t):
        steps = []
        for u in range(UNROLL):
            run, a, b = (items[w, t * UNROLL + u] for w in range(3))
            a, b = a + base, b + base
            k = jnp.concatenate([keys_of(kv, a), keys_of(kv, b)], axis=0)
            k = jnp.concatenate([k, k], axis=1)
            v = jnp.concatenate(values_of(kv, a) + values_of(kv, b), axis=1)
            steps += [(k, v, run, slice(j * TILE, (j + 1) * TILE)) for j in range(PER // TILE)]

        def score(i):
            k, _, run, cols = steps[i]
            return jnp.dot(k, qt[run, :, cols], preferred_element_type=F32)

        s = score(0)
        for i, (_, v, run, cols) in enumerate(steps):
            later = score(i + 1) if i + 1 < len(steps) else None
            x = s - mref[run, :, cols]
            viol[run, :, cols] = jnp.maximum(viol[run, :, cols], jnp.max(x.reshape(2 * RUN // 8, 8, TILE), axis=0))
            p = jnp.exp2(x).astype(BF16)
            acc[run, :, cols] += jnp.dot(v, p, preferred_element_type=F32)
            s = later


def read_ranks(copies, kv, base, count, ranks):
    each = count // len(copies)
    for i, copy in enumerate(copies):
        copy.wait()
        for s in range(i * each, (i + 1) * each):
            ranks[s] = jnp.max(kv[base + s, 512:528, :].astype(F32)).astype(I32)


def fill(kv, base, sources, sems):
    copies = []
    for i, src in enumerate(sources):
        copy = pltpu.make_async_copy(src, kv.at[pl.ds(base, src.shape[0])], sems.at[i])
        copy.start()
        copies.append(copy)
        base += src.shape[0]
    return copies


def set_ones(kv, first, count):
    kv[pl.ds(first, count), 512:528, :] = jnp.ones((count, 16, D), BF16)


def turn_kernel(q0, q1, qt):
    for i in range(4):
        for h in range(4):
            rows = slice(i // 2 * RUN, (i // 2 + 1) * RUN)
            block = (q0, q1)[i % 2][rows, h * D : (h + 1) * D].astype(F32).T * SCALE
            high = block.astype(BF16)
            here = slice(h * RUN, (h + 1) * RUN)
            qt[i, 0:D, here] = high
            qt[i, D : 2 * D, here] = (block - high.astype(F32)).astype(BF16)


def early_kernel(qt, s0, s1, ranks, mref, acc, viol, kv, items, sems):
    read_ranks(fill(kv, 0, (s0, s1), sems), kv, 0, PART, ranks)
    n = jnp.int32(0)
    for i in range(4):
        n = work_list(items, ranks, PART, ranks[OWN[i]], i, n)
    set_ones(kv, 0, PART)
    kv[PART] = jnp.zeros((ROWS, D), BF16)
    key = lax.broadcasted_iota(I32, (RUN, PER), 0)
    query = lax.broadcasted_iota(I32, (RUN, PER), 1) % RUN
    keep = key <= query
    for i in range(4):
        k = keys_of(kv, OWN[i])
        s = jnp.dot(jnp.concatenate([k, k], axis=1), qt[i], preferred_element_type=F32)
        s = jnp.where(keep, s, -1e30)
        top = jnp.max(s, axis=0, keepdims=True)
        mref[i] = top
        p = jnp.exp2(s - top).astype(BF16)
        v = jnp.concatenate(values_of(kv, OWN[i]), axis=1)
        acc[i] = jnp.dot(v, p, preferred_element_type=F32)
    viol[...] = jnp.zeros_like(viol)
    absorb_items(items, n, kv, 0, PART, qt, mref, acc, viol)


def take_state(state, held, first, count, sems):
    copies = []
    for i, (src, dst) in enumerate(zip(state, held)):
        copy = pltpu.make_async_copy(src.at[pl.ds(first, count)], dst, sems.at[i])
        copy.start()
        copies.append(copy)
    return copies


def middle_kernel(early_ranks, qt, mref, acc_in, viol_in, s0, s1, ranks, acc, viol, kv, items, sems):
    copies = fill(kv, 0, (s0, s1), sems)
    acc[...] = acc_in[...]
    viol[...] = viol_in[...]
    read_ranks(copies, kv, 0, PART, ranks)
    n = jnp.int32(0)
    for i in range(4):
        n = work_list(items, ranks, PART, early_ranks[OWN[i]], i, n)
    set_ones(kv, 0, PART)
    kv[PART] = jnp.zeros((ROWS, D), BF16)
    absorb_items(items, n, kv, 0, PART, qt, mref, acc, viol)


def late_kernel(chunk, early_ranks, middle_ranks, *rest):
    state, sources = rest[:4], rest[4:12]
    *out, kv, qt, mref, acc, viol, ranks, items, sems, state_sems = rest[12:]
    base, count = 2 * PART, 2 * PART
    copies = fill(kv, base, sources[4:], sems)
    state_copies = take_state(state, (qt, mref, acc, viol), 2 * chunk, 2, state_sems)
    read_ranks(copies, kv, base, count, ranks)
    n = jnp.int32(0)
    for i in range(2):
        n = work_list(items, ranks, count, early_ranks[OWN[2 * chunk + i]], i, n)
    set_ones(kv, base, count)
    kv[base + count] = jnp.zeros((ROWS, D), BF16)
    for copy in state_copies:
        copy.wait()
    absorb_items(items, n, kv, base, count, qt, mref, acc, viol)

    @pl.when(jnp.max(viol[...]) > LIMIT)
    def _():
        for copy in fill(kv, 0, sources[:4], sems):
            copy.wait()
        set_ones(kv, 0, base)
        later = lax.broadcasted_iota(I32, (RUN, RUN), 0) > lax.broadcasted_iota(I32, (RUN, RUN), 1)

        def take(slot, slot_rank, run, rank, cols):
            @pl.when(slot_rank <= rank)
            def _():
                k = keys_of(kv, slot)
                s = jnp.dot(jnp.concatenate([k, k], axis=1), qt[run, :, cols], preferred_element_type=F32)
                drop = jnp.logical_and(later, jnp.full((RUN, RUN), slot_rank, I32) == rank)
                s = jnp.where(drop, -1e30, s)
                old = viol[run, 0:1, cols]
                top = jnp.maximum(old, jnp.max(s, axis=0, keepdims=True))
                viol[run, 0:1, cols] = top
                p = jnp.exp2(s - top).astype(BF16)
                v = jnp.concatenate(values_of(kv, slot), axis=1)
                term = jnp.dot(v, p, preferred_element_type=F32)
                acc[run, :, cols] = acc[run, :, cols] * jnp.exp2(old - top) + term

        @pl.loop(0, 2 * PER // RUN)
        def _(t):
            run = t // (PER // RUN)
            cols = pl.ds(pl.multiple_of(t % (PER // RUN) * RUN, RUN), RUN)
            rank = jnp.where(run == 0, early_ranks[OWN[2 * chunk]], early_ranks[OWN[2 * chunk + 1]])
            acc[run, :, cols] = jnp.zeros((144, RUN), F32)
            viol[run, :, cols] = jnp.full((8, RUN), -1e30, F32)
            for first, held, many in ((0, early_ranks, PART), (PART, middle_ranks, PART), (base, ranks, count)):

                @pl.loop(0, many)
                def _(s, first=first, held=held):
                    take(first + s, held[s], run, rank, cols)

    for i in range(2):
        for h in range(4):
            cols = slice(h * RUN, (h + 1) * RUN)
            block = acc[i, 0:D, cols] / acc[i, D : D + 1, cols]
            out[i][:, h * D : (h + 1) * D] = block.T.astype(BF16)


def spec(space):
    return pl.BlockSpec(memory_space=space)


def cost(slots, runs):
    pairs = slots * RUN * runs * PER // 2
    return pl.CostEstimate(flops=8 * D * pairs, bytes_accessed=12 * 10**6, transcendentals=pairs)


RANKS = jax.ShapeDtypeStruct((PART,), I32)
def held(runs):
    return [pltpu.VMEM((runs, 2 * D, PER), BF16), pltpu.VMEM((runs, 1, PER), F32)]


STATE = (jax.ShapeDtypeStruct((4, 144, PER), F32), jax.ShapeDtypeStruct((4, 8, PER), F32))
PARAMS = pltpu.CompilerParams(vmem_limit_bytes=VMEM)
SMALL = pltpu.CompilerParams(vmem_limit_bytes=12 * 2**20)


def lists(slots):
    return [pltpu.SMEM((3, 2 * slots + 16), I32)]


def turn(q0, q1):
    return pl.pallas_call(
        turn_kernel,
        name="turn_queries",
        out_shape=jax.ShapeDtypeStruct((4, 2 * D, PER), BF16),
        in_specs=[spec(pltpu.VMEM)] * 2,
        out_specs=spec(pltpu.VMEM),
        compiler_params=SMALL,
        cost_estimate=pl.CostEstimate(flops=10**7, bytes_accessed=3 * 10**6, transcendentals=0),
    )(q0, q1)


def attend_early(qt, pieces):
    return pl.pallas_call(
        early_kernel,
        name="attend_early",
        out_shape=(RANKS, jax.ShapeDtypeStruct((4, 1, PER), F32)) + STATE,
        in_specs=[spec(pltpu.VMEM)] + [spec(pl.ANY)] * 2,
        out_specs=(spec(pltpu.SMEM),) + (spec(pltpu.VMEM),) * 3,
        scratch_shapes=[pltpu.VMEM((PART + 1, ROWS, D), BF16), *lists(PART), pltpu.SemaphoreType.DMA((2,))],
        compiler_params=PARAMS,
        cost_estimate=cost(PART, 4),
    )(qt, *pieces)


def attend_middle(early_ranks, state, pieces):
    return pl.pallas_call(
        middle_kernel,
        name="attend_middle",
        out_shape=(RANKS,) + STATE,
        in_specs=[spec(pltpu.SMEM)] + [spec(pltpu.VMEM)] * 4 + [spec(pl.ANY)] * 2,
        out_specs=(spec(pltpu.SMEM),) + (spec(pltpu.VMEM),) * 2,
        scratch_shapes=[pltpu.VMEM((PART + 1, ROWS, D), BF16), *lists(PART), pltpu.SemaphoreType.DMA((2,))],
        compiler_params=PARAMS,
        cost_estimate=cost(PART, 4),
    )(early_ranks, *state, *pieces)


def attend_late(ranks, state, pieces, chunk):
    return pl.pallas_call(
        functools.partial(late_kernel, chunk),
        name="attend_late",
        out_shape=(jax.ShapeDtypeStruct((RUN, 4 * D), BF16),) * 2,
        in_specs=[spec(pltpu.SMEM)] * 2 + [spec(pl.ANY)] * 12,
        out_specs=(spec(pltpu.VMEM),) * 2,
        scratch_shapes=[
            pltpu.VMEM((4 * PART + 1, ROWS, D), BF16),
            *held(2),
            pltpu.VMEM((2, 144, PER), F32),
            pltpu.VMEM((2, 8, PER), F32),
            pltpu.SMEM((2 * PART,), I32),
            *lists(2 * PART),
            pltpu.SemaphoreType.DMA((4,)),
            pltpu.SemaphoreType.DMA((4,)),
        ],
        compiler_params=PARAMS,
        cost_estimate=cost(2 * PART, 2),
    )(*ranks, *state, *pieces)


def project_kernel(place, even, a0, a1, b0, b1, w_own, w0, w1, w2, w3, out, rows):
    width = w0.shape[1]
    half = a0.shape[1]
    for swap in (0, 1):

        @pl.when(even[0] == 1 - swap)
        def _(swap=swap):
            for i, pair in enumerate(((a0, a1), (b0, b1))):
                rows[i, :, 0:half] = pair[swap][...]
                rows[i, :, half : 2 * half] = pair[1 - swap][...]

    for e, w in enumerate((w0, w1, w2, w3)):
        for j in range(width // SHARE):
            at = pl.ds(pl.multiple_of(place[e] * width + j * SHARE, SHARE), SHARE)
            term = jnp.dot(rows[0], w_own[:, at], preferred_element_type=F32)
            term = term + jnp.dot(rows[1], w[:, j * SHARE : (j + 1) * SHARE], preferred_element_type=F32)
            out[:, at] = term.astype(BF16)


def project(place, even, got, w_own, shares):
    rows, depth = got[0].shape[0], w_own.shape[0]
    width = w_own.shape[1]
    return pl.pallas_call(
        project_kernel,
        name="project",
        out_shape=jax.ShapeDtypeStruct((rows, width), BF16),
        in_specs=[spec(pltpu.SMEM)] * 2 + [spec(pltpu.VMEM)] * 9,
        out_specs=spec(pltpu.VMEM),
        scratch_shapes=[pltpu.VMEM((2, rows, depth), BF16)],
        compiler_params=PARAMS,
        cost_estimate=pl.CostEstimate(
            flops=4 * rows * depth * width, bytes_accessed=20 * 10**6, transcendentals=0
        ),
    )(place, even, *got, w_own, *shares)


def finish_kernel(a, b, *rest):
    rest[-1][...] = (a[...].astype(F32) + b[...].astype(F32)).astype(BF16)


def finish(a, b, chunk, before=None):
    rows, width = a.shape
    whole = pl.BlockSpec((rows // 4, width), lambda i: (i, 0))
    more = {} if before is None else {"input_output_aliases": {2: 0}}
    extra = [] if before is None else [before]
    return pl.pallas_call(
        finish_kernel,
        name="finish",
        grid=(4,),
        out_shape=jax.ShapeDtypeStruct((2 * rows, width), BF16),
        in_specs=[whole, whole] + [spec(pl.ANY)] * len(extra),
        out_specs=pl.BlockSpec((rows // 4, width), lambda i: (4 * chunk + i, 0)),
        compiler_params=SMALL,
        **more,
    )(a, b, *extra)


def body(queries, keys, values, positions, out_weight):
    xl, c = lax.axis_index("xl"), lax.axis_index("c")
    y, z = lax.axis_index("y"), lax.axis_index("z")
    rank = (positions.reshape(2, RUN)[:, 0] // RUN).astype(BF16)
    turned = values.reshape(2, 2, D, D).transpose(0, 1, 3, 2).reshape(2, RUN, D)
    marks = jnp.broadcast_to(rank[:, None, None], (2, 16, D))
    piece = jnp.concatenate([keys.reshape(2, RUN, D), turned, marks], axis=1)
    width = out_weight.shape[1] // 8
    line, bit = jnp.where(c == 0, y, z), jnp.where(c == 0, z, y) % 2
    share = lax.dynamic_slice_in_dim(out_weight, (line * 2 + bit) * width, width, 1)
    piece = route(piece, lambda y, xl, z, xh, c: (y, c, z, xh, xl))
    share = route(share, lambda y, xl, z, xh, c: (y, 1 - xl, z, 1 - xh, c))
    q = []
    for k in (0, 1):
        half = lax.dynamic_slice_in_dim(queries, (xl ^ k) * 4 * D, 4 * D, 1)
        q.append(route(half, lambda y, xl, z, xh, c, k=k: (y, c, z, xh, xl ^ k)))
    near = jnp.concatenate([piece] + [onward(piece, d, 0) for d in SHIFTS[1:]])
    near, q = lax.optimization_barrier((near, q))
    pieces = [near, other_core(near)]
    side = [onward(near, d, 1) for d in SHIFTS[1:]]
    qt = turn(*q)
    ranks, mref, acc, viol = attend_early(qt, pieces)
    side, acc, share = lax.optimization_barrier((side, acc, share))
    other = [other_core(b) for b in side]
    pair = route(share, lambda y, xl, z, xh, c: (y ^ c, xl, z ^ (1 - c), xh, c))
    more, acc, viol = attend_middle(ranks, (qt, mref, acc, viol), side[:2])
    other, acc, share, pair = lax.optimization_barrier((other, acc, share, pair))
    share = jnp.concatenate([jnp.where(bit == 0, share, pair), jnp.where(bit == 0, pair, share)], axis=1)
    shares = [share] + [onward(share, d, 1) for d in (1, 3)]
    pieces = [*pieces, *side, *other]
    place = (line - jnp.array(SHIFTS, I32)) % 4
    even = (xl == 0).astype(I32).reshape(1)
    state = (qt, mref, acc, viol)
    out = None
    for chunk in (0, 1):
        attended = attend_late((ranks, more), state, pieces, chunk)
        got = [
            route(attended[k], lambda y, xl, z, xh, c, k=k, far=far: (y, c ^ k, z, xh ^ far, xl))
            for far in (0, 1)
            for k in (0, 1)
        ]
        if chunk == 0:
            attended, state, shares = lax.optimization_barrier((attended, state, shares))
            shares.append(onward(shares[0], 2, 1))
        part = project(place, even, got, out_weight, shares)
        out = finish(part, other_core(part), chunk, out)
    return out


def solution(mesh):
    fine = Mesh(mesh.devices.reshape(SIZES), AXES)
    tokens, heads = ("y", "xl", "z"), ("xh", "c")
    placed = (P(tokens, heads), P(tokens, heads), P(tokens, heads), P(tokens), P(heads, None))
    return jax.shard_map(body, mesh=fine, in_specs=placed, out_specs=P(tokens, None), check_vma=False)
```

```python
import functools
import math

import jax
import jax.numpy as jnp
import numpy as np
from jax import lax
from jax.experimental import pallas as pl
from jax.experimental.pallas import tpu as pltpu
from jax.sharding import Mesh
from jax.sharding import PartitionSpec as P

D = 128
RUN = 256
AXES = ("y", "xl", "z", "xh", "c")
SIZES = (4, 2, 4, 2, 2)
SCALE = math.log2(math.e) / math.sqrt(D)
ROWS = 528
NQ = 4096
PER = 1024
TILE = 512
UNROLL = 4
LIMIT = 100.0
SHIFTS = (0, 1, 3, 2)
SHARE = 256
SHARE = 256
OWN = (0, 8, 1, 9)
VMEM = 28 * 2**20
PART = 16
PER = 1024
TILE = 512
UNROLL = 4
LIMIT = 100.0
SHIFTS = (0, 1, 3, 2)
SHARE = 256
OWN = (0, 8, 1, 9)
VMEM = 28 * 2**20
F32, BF16, I32 = jnp.float32, jnp.bfloat16, jnp.int32


def route(block, f):
    pairs = [
        (int(np.ravel_multi_index(i, SIZES)), int(np.ravel_multi_index(f(*i), SIZES)))
        for i in np.ndindex(*SIZES)
    ]
    return lax.ppermute(block, AXES, pairs)


def onward(block, d, stage):
    def f(y, xl, z, xh, c):
        return (y, xl, (z + d) % 4, xh, c) if c == stage else ((y + d) % 4, xl, z, xh, c)

    return route(block, f)


def other_core(block):
    return route(block, lambda y, xl, z, xh, c: (y, xl, z, xh, 1 - c))


def values_of(kv, slot):
    ones = kv[slot, 512:528, :]
    return [jnp.concatenate([kv[slot, 256 + 128 * h : 384 + 128 * h, :], ones], axis=0) for h in (0, 1)]


def keys_of(kv, slot):
    return kv[slot, 0:256, :]


def work_list(items, ranks, count, rank, run, n):
    found = jnp.int32(0)
    for s in range(count):
        items[0, n + (found >> 1)] = run
        items[1 + (found & 1), n + (found >> 1)] = s
        found = found + (ranks[s] < rank).astype(I32)
    items[1 + (found & 1), n + (found >> 1)] = count
    return n + ((found + 1) >> 1)


def absorb_items(items, n, kv, base, count, qt, mref, acc, viol):
    for u in range(UNROLL):
        items[0, n + u] = 0
        items[1, n + u] = count
        items[2, n + u] = count

    @pl.loop(0, (n + UNROLL - 1) // UNROLL)
    def _(t):
        steps = []
        for u in range(UNROLL):
            run, a, b = (items[w, t * UNROLL + u] for w in range(3))
            a, b = a + base, b + base
            k = jnp.concatenate([keys_of(kv, a), keys_of(kv, b)], axis=0)
            k = jnp.concatenate([k, k], axis=1)
            v = jnp.concatenate(values_of(kv, a) + values_of(kv, b), axis=1)
            steps += [(k, v, run, slice(j * TILE, (j + 1) * TILE)) for j in range(PER // TILE)]

        def score(i):
            k, _, run, cols = steps[i]
            return jnp.dot(k, qt[run, :, cols], preferred_element_type=F32)

        s = score(0)
        for i, (_, v, run, cols) in enumerate(steps):
            later = score(i + 1) if i + 1 < len(steps) else None
            x = s - mref[run, :, cols]
            viol[run, :, cols] = jnp.maximum(viol[run, :, cols], jnp.max(x.reshape(2 * RUN // 8, 8, TILE), axis=0))
            p = jnp.exp2(x).astype(BF16)
            acc[run, :, cols] += jnp.dot(v, p, preferred_element_type=F32)
            s = later


def read_ranks(copies, kv, base, count, ranks):
    each = count // len(copies)
    for i, copy in enumerate(copies):
        copy.wait()
        for s in range(i * each, (i + 1) * each):
            ranks[s] = jnp.max(kv[base + s, 512:528, :].astype(F32)).astype(I32)


def fill(kv, base, sources, sems):
    copies = []
    for i, src in enumerate(sources):
        copy = pltpu.make_async_copy(src, kv.at[pl.ds(base, src.shape[0])], sems.at[i])
        copy.start()
        copies.append(copy)
        base += src.shape[0]
    return copies


def set_ones(kv, first, count):
    kv[pl.ds(first, count), 512:528, :] = jnp.ones((count, 16, D), BF16)


def pack_kernel(positions, keys, values, out):
    for r in range(2):
        out[r, 0:RUN, :] = keys[r * RUN : (r + 1) * RUN, :]
        for h in range(2):
            block = values[r * RUN + h * D : r * RUN + (h + 1) * D, :].astype(F32)
            out[r, RUN + h * D : RUN + (h + 1) * D, :] = block.T.astype(BF16)
        rank = (positions[r * RUN] >> 8).astype(F32)
        out[r, 2 * RUN : ROWS, :] = jnp.full((16, D), rank, F32).astype(BF16)


def turn_kernel(q0, q1, qt, token):
    token[0] = jnp.int32(0)
    for i in range(4):
        for h in range(4):
            rows = slice(i // 2 * RUN, (i // 2 + 1) * RUN)
            block = (q0, q1)[i % 2][rows, h * D : (h + 1) * D].astype(F32).T * SCALE
            high = block.astype(BF16)
            here = slice(h * RUN, (h + 1) * RUN)
            qt[i, 0:D, here] = high
            qt[i, D : 2 * D, here] = (block - high.astype(F32)).astype(BF16)


def early_kernel(token, qt, s0, s1, ranks, mref, acc, viol, kv, items, sems):
    read_ranks(fill(kv, 0, (s0, s1), sems), kv, 0, PART, ranks)
    n = jnp.int32(0)
    for i in range(4):
        n = work_list(items, ranks, PART, ranks[OWN[i]], i, n)
    set_ones(kv, 0, PART)
    kv[PART] = jnp.zeros((ROWS, D), BF16)
    key = lax.broadcasted_iota(I32, (RUN, PER), 0)
    query = lax.broadcasted_iota(I32, (RUN, PER), 1) % RUN
    keep = key <= query
    for i in range(4):
        k = keys_of(kv, OWN[i])
        s = jnp.dot(jnp.concatenate([k, k], axis=1), qt[i], preferred_element_type=F32)
        s = jnp.where(keep, s, -1e30)
        top = jnp.max(s, axis=0, keepdims=True)
        mref[i] = top
        p = jnp.exp2(s - top).astype(BF16)
        v = jnp.concatenate(values_of(kv, OWN[i]), axis=1)
        acc[i] = jnp.dot(v, p, preferred_element_type=F32)
    viol[...] = jnp.zeros_like(viol)
    absorb_items(items, n, kv, 0, PART, qt, mref, acc, viol)


def take_state(state, held, first, count, sems):
    copies = []
    for i, (src, dst) in enumerate(zip(state, held)):
        copy = pltpu.make_async_copy(src.at[pl.ds(first, count)], dst, sems.at[i])
        copy.start()
        copies.append(copy)
    return copies


def middle_kernel(early_ranks, qt, mref, acc_in, viol_in, s0, s1, ranks, acc, viol, kv, items, sems):
    copies = fill(kv, 0, (s0, s1), sems)
    acc[...] = acc_in[...]
    viol[...] = viol_in[...]
    read_ranks(copies, kv, 0, PART, ranks)
    n = jnp.int32(0)
    for i in range(4):
        n = work_list(items, ranks, PART, early_ranks[OWN[i]], i, n)
    set_ones(kv, 0, PART)
    kv[PART] = jnp.zeros((ROWS, D), BF16)
    absorb_items(items, n, kv, 0, PART, qt, mref, acc, viol)


def late_kernel(chunk, early_ranks, middle_ranks, *rest):
    state, sources = rest[:4], rest[4:12]
    *out, kv, qt, mref, acc, viol, ranks, items, sems, state_sems = rest[12:]
    base, count = 2 * PART, 2 * PART
    copies = fill(kv, base, sources[4:], sems)
    state_copies = take_state(state, (qt, mref, acc, viol), 2 * chunk, 2, state_sems)
    read_ranks(copies, kv, base, count, ranks)
    n = jnp.int32(0)
    for i in range(2):
        n = work_list(items, ranks, count, early_ranks[OWN[2 * chunk + i]], i, n)
    set_ones(kv, base, count)
    kv[base + count] = jnp.zeros((ROWS, D), BF16)
    for copy in state_copies:
        copy.wait()
    absorb_items(items, n, kv, base, count, qt, mref, acc, viol)

    @pl.when(jnp.max(viol[...]) > LIMIT)
    def _():
        for copy in fill(kv, 0, sources[:4], sems):
            copy.wait()
        set_ones(kv, 0, base)
        later = lax.broadcasted_iota(I32, (RUN, RUN), 0) > lax.broadcasted_iota(I32, (RUN, RUN), 1)

        def take(slot, slot_rank, run, rank, cols):
            @pl.when(slot_rank <= rank)
            def _():
                k = keys_of(kv, slot)
                s = jnp.dot(jnp.concatenate([k, k], axis=1), qt[run, :, cols], preferred_element_type=F32)
                drop = jnp.logical_and(later, jnp.full((RUN, RUN), slot_rank, I32) == rank)
                s = jnp.where(drop, -1e30, s)
                old = viol[run, 0:1, cols]
                top = jnp.maximum(old, jnp.max(s, axis=0, keepdims=True))
                viol[run, 0:1, cols] = top
                p = jnp.exp2(s - top).astype(BF16)
                v = jnp.concatenate(values_of(kv, slot), axis=1)
                term = jnp.dot(v, p, preferred_element_type=F32)
                acc[run, :, cols] = acc[run, :, cols] * jnp.exp2(old - top) + term

        @pl.loop(0, 2 * PER // RUN)
        def _(t):
            run = t // (PER // RUN)
            cols = pl.ds(pl.multiple_of(t % (PER // RUN) * RUN, RUN), RUN)
            rank = jnp.where(run == 0, early_ranks[OWN[2 * chunk]], early_ranks[OWN[2 * chunk + 1]])
            acc[run, :, cols] = jnp.zeros((144, RUN), F32)
            viol[run, :, cols] = jnp.full((8, RUN), -1e30, F32)
            for first, held, many in ((0, early_ranks, PART), (PART, middle_ranks, PART), (base, ranks, count)):

                @pl.loop(0, many)
                def _(s, first=first, held=held):
                    take(first + s, held[s], run, rank, cols)

    for i in range(2):
        for h in range(4):
            cols = slice(h * RUN, (h + 1) * RUN)
            block = acc[i, 0:D, cols] / acc[i, D : D + 1, cols]
            out[i][:, h * D : (h + 1) * D] = block.T.astype(BF16)


def spec(space):
    return pl.BlockSpec(memory_space=space)


def cost(slots, runs):
    pairs = slots * RUN * runs * PER // 2
    return pl.CostEstimate(flops=8 * D * pairs, bytes_accessed=12 * 10**6, transcendentals=pairs)


RANKS = jax.ShapeDtypeStruct((PART,), I32)
def held(runs):
    return [pltpu.VMEM((runs, 2 * D, PER), BF16), pltpu.VMEM((runs, 1, PER), F32)]


STATE = (jax.ShapeDtypeStruct((4, 144, PER), F32), jax.ShapeDtypeStruct((4, 8, PER), F32))
PARAMS = pltpu.CompilerParams(vmem_limit_bytes=VMEM)
LARGE = pltpu.CompilerParams(vmem_limit_bytes=56 * 2**20)
SMALL = pltpu.CompilerParams(vmem_limit_bytes=12 * 2**20)


def lists(slots):
    return [pltpu.SMEM((3, 2 * slots + 16), I32)]


def pack(positions, keys, values):
    return pl.pallas_call(
        pack_kernel,
        name="pack",
        out_shape=jax.ShapeDtypeStruct((2, ROWS, D), BF16),
        in_specs=[spec(pltpu.SMEM)] + [spec(pltpu.VMEM)] * 2,
        out_specs=spec(pltpu.VMEM),
        compiler_params=SMALL,
    )(positions, keys, values)


def turn(q0, q1):
    return pl.pallas_call(
        turn_kernel,
        name="turn_queries",
        out_shape=(jax.ShapeDtypeStruct((4, 2 * D, PER), BF16), jax.ShapeDtypeStruct((1,), I32)),
        in_specs=[spec(pltpu.VMEM)] * 2,
        out_specs=(spec(pltpu.VMEM), spec(pltpu.SMEM)),
        compiler_params=SMALL,
        cost_estimate=pl.CostEstimate(flops=10**7, bytes_accessed=3 * 10**6, transcendentals=0),
    )(q0, q1)


def attend_early(token, qt, pieces):
    return pl.pallas_call(
        early_kernel,
        name="attend_early",
        out_shape=(RANKS, jax.ShapeDtypeStruct((4, 1, PER), F32)) + STATE,
        in_specs=[spec(pltpu.SMEM), spec(pltpu.VMEM)] + [spec(pl.ANY)] * 2,
        out_specs=(spec(pltpu.SMEM),) + (spec(pltpu.VMEM),) * 3,
        scratch_shapes=[pltpu.VMEM((PART + 1, ROWS, D), BF16), *lists(PART), pltpu.SemaphoreType.DMA((2,))],
        compiler_params=PARAMS,
        cost_estimate=cost(PART, 4),
    )(token, qt, *pieces)


def attend_middle(early_ranks, state, pieces):
    return pl.pallas_call(
        middle_kernel,
        name="attend_middle",
        out_shape=(RANKS,) + STATE,
        in_specs=[spec(pltpu.SMEM)] + [spec(pltpu.VMEM)] * 4 + [spec(pl.ANY)] * 2,
        out_specs=(spec(pltpu.SMEM),) + (spec(pltpu.VMEM),) * 2,
        scratch_shapes=[pltpu.VMEM((PART + 1, ROWS, D), BF16), *lists(PART), pltpu.SemaphoreType.DMA((2,))],
        compiler_params=PARAMS,
        cost_estimate=cost(PART, 4),
    )(early_ranks, *state, *pieces)


def attend_late(ranks, state, pieces, chunk):
    return pl.pallas_call(
        functools.partial(late_kernel, chunk),
        name="attend_late",
        out_shape=(jax.ShapeDtypeStruct((RUN, 4 * D), BF16),) * 2,
        in_specs=[spec(pltpu.SMEM)] * 2 + [spec(pl.ANY)] * 12,
        out_specs=(spec(pltpu.VMEM),) * 2,
        scratch_shapes=[
            pltpu.VMEM((4 * PART + 1, ROWS, D), BF16),
            *held(2),
            pltpu.VMEM((2, 144, PER), F32),
            pltpu.VMEM((2, 8, PER), F32),
            pltpu.SMEM((2 * PART,), I32),
            *lists(2 * PART),
            pltpu.SemaphoreType.DMA((4,)),
            pltpu.SemaphoreType.DMA((4,)),
        ],
        compiler_params=LARGE,
        cost_estimate=cost(2 * PART, 2),
    )(*ranks, *state, *pieces)


def project_kernel(place, even, a0, a1, b0, b1, w_own, w0, w1, w2, w3, out, rows):
    width = w0.shape[1]
    half = a0.shape[1]
    for swap in (0, 1):

        @pl.when(even[0] == 1 - swap)
        def _(swap=swap):
            for i, pair in enumerate(((a0, a1), (b0, b1))):
                rows[i, :, 0:half] = pair[swap][...]
                rows[i, :, half : 2 * half] = pair[1 - swap][...]

    for e, w in enumerate((w0, w1, w2, w3)):
        for j in range(width // SHARE):
            half_width = width // 2
            first, rest = divmod(j * SHARE, half_width)
            at = pl.ds(pl.multiple_of(place[2 * e + first] * half_width + rest, SHARE), SHARE)
            term = jnp.dot(rows[0], w_own[:, at], preferred_element_type=F32)
            term = term + jnp.dot(rows[1], w[:, j * SHARE : (j + 1) * SHARE], preferred_element_type=F32)
            out[:, at] = term.astype(BF16)


def project(place, even, got, w_own, shares):
    rows, depth = got[0].shape[0], w_own.shape[0]
    width = w_own.shape[1]
    return pl.pallas_call(
        project_kernel,
        name="project",
        out_shape=jax.ShapeDtypeStruct((rows, width), BF16),
        in_specs=[spec(pltpu.SMEM)] * 2 + [spec(pltpu.VMEM)] * 9,
        out_specs=spec(pltpu.VMEM),
        scratch_shapes=[pltpu.VMEM((2, rows, depth), BF16)],
        compiler_params=PARAMS,
        cost_estimate=pl.CostEstimate(
            flops=4 * rows * depth * width, bytes_accessed=20 * 10**6, transcendentals=0
        ),
    )(place, even, *got, w_own, *shares)


def finish_kernel(a, b, *rest):
    rest[-1][...] = (a[...].astype(F32) + b[...].astype(F32)).astype(BF16)


def finish(a, b, chunk, before=None):
    rows, width = a.shape
    whole = pl.BlockSpec((rows // 4, width), lambda i: (i, 0))
    more = {} if before is None else {"input_output_aliases": {2: 0}}
    extra = [] if before is None else [before]
    return pl.pallas_call(
        finish_kernel,
        name="finish",
        grid=(4,),
        out_shape=jax.ShapeDtypeStruct((2 * rows, width), BF16),
        in_specs=[whole, whole] + [spec(pl.ANY)] * len(extra),
        out_specs=pl.BlockSpec((rows // 4, width), lambda i: (4 * chunk + i, 0)),
        compiler_params=SMALL,
        **more,
    )(a, b, *extra)


def body(queries, keys, values, positions, out_weight):
    xl, c = lax.axis_index("xl"), lax.axis_index("c")
    y, z = lax.axis_index("y"), lax.axis_index("z")
    piece = pack(positions, keys, values)
    width = out_weight.shape[1] // 8
    line, bit = jnp.where(c == 0, y, z), jnp.where(c == 0, z, y) % 2
    share = lax.dynamic_slice_in_dim(out_weight, (line * 2 + bit) * width, width, 1)
    piece = route(piece, lambda y, xl, z, xh, c: (y, c, z, xh, xl))
    share = route(share, lambda y, xl, z, xh, c: (y, 1 - xl, z, 1 - xh, c))
    q = []
    for k in (0, 1):
        half = lax.dynamic_slice_in_dim(queries, (xl ^ k) * 4 * D, 4 * D, 1)
        q.append(route(half, lambda y, xl, z, xh, c, k=k: (y, c, z, xh, xl ^ k)))
    near = jnp.concatenate([piece] + [onward(piece, d, 0) for d in SHIFTS[1:]])
    qt, token = turn(*q)
    near, token = lax.optimization_barrier((near, token))
    pieces = [near, other_core(near)]
    side = [onward(near, d, 1) for d in SHIFTS[1:]]
    ranks, mref, acc, viol = attend_early(token, qt, pieces)
    side, acc, share = lax.optimization_barrier((side, acc, share))
    other = [other_core(b) for b in side]
    pair = route(share, lambda y, xl, z, xh, c: (y ^ c, xl, z ^ (1 - c), xh, c))
    more, acc, viol = attend_middle(ranks, (qt, mref, acc, viol), side[:2])
    other, acc, share, pair = lax.optimization_barrier((other, acc, share, pair))
    share = jnp.concatenate([share, pair], axis=1)
    shares = [share] + [onward(share, d, 1) for d in (1, 3)]
    pieces = [*pieces, *side, *other]
    place = (2 * ((line - jnp.array(SHIFTS, I32)) % 4)[:, None] + jnp.stack([bit, 1 - bit])[None, :]).reshape(8)
    even = (xl == 0).astype(I32).reshape(1)
    state = (qt, mref, acc, viol)
    out = None
    for chunk in (0, 1):
        attended = attend_late((ranks, more), state, pieces, chunk)
        got = [
            route(attended[k], lambda y, xl, z, xh, c, k=k, far=far: (y, c ^ k, z, xh ^ far, xl))
            for far in (0, 1)
            for k in (0, 1)
        ]
        if chunk == 0:
            attended, state, shares = lax.optimization_barrier((attended, state, shares))
            shares.append(onward(shares[0], 2, 1))
        part = project(place, even, got, out_weight, shares)
        out = finish(part, other_core(part), chunk, out)
    return out


def solution(mesh):
    fine = Mesh(mesh.devices.reshape(SIZES), AXES)
    tokens, heads = ("y", "xl", "z"), ("xh", "c")
    placed = (P(tokens, heads), P(tokens, heads), P(tokens, heads), P(tokens), P(heads, None))
    return jax.shard_map(body, mesh=fine, in_specs=placed, out_specs=P(tokens, None), check_vma=False)
```
